32 devices in a mesh: section: 2 (over core), shard: 16 (over z, y, x).
Axes of the slice: x: 2, y: 2, z: 4, core: 2. Of those that a mesh axis runs over, the one named last changes fastest.
Arguments:
- hidden: bfloat16 [64, 32, 768], P('shard', None, 'section'), may hold values from -6 to 6
- proj: bfloat16 [768, 128], P('section'), may hold values from -0.21875 to 0.21875
- passages: bfloat16 [2048, 180, 128], P('shard'), may hold values from -24 to 24
- pass_len: int32 [2048], P('shard'), may hold values from 45 to 180
- query_len: int32 [64], P('shard'), may hold values from 8 to 32
- cand_owner: int32 [2, 64, 32, 1], P('section', 'shard'), may hold values from 0 to 15; in each aligned block of 128 rows (0 to 127, 128 to 255, ..., all dimensions but the last counted through in order) at most 16 rows name the same one
- cand_slot: int32 [2, 64, 32], P('section', 'shard'), may hold values from 0 to 127
- teacher: float32 [64, 64], P('shard', 'section'), may hold values from -18 to 318
Outputs:
- kl_div: float32 [64], P('shard')
- grad_hidden: bfloat16 [64, 32, 768], P('shard', None, 'section')
- grad_proj: float32 [768, 128], P('section')
The draws below stay inside these ranges and needn't reach their ends.
Inputs may be any that keep to these rules, and one draw needn't show every extreme that they name: `cand_owner`: among the 128 candidates held by one device (one index of section, the queries of one index of shard), at most 16 name any one owner.
All inputs are finite; a program needn't handle non-finite values.
Results may differ from the reference program's by a relative error of at most 0.022.
Values may be sent and summed in bfloat16 or wider, within the bound.
A program may use at most 128 MiB of HBM per device.

```python
import math
import jax
import jax.numpy as jnp
import numpy as np
from jax import lax

D = 768
DV = 128
QLEN = 32
PLEN = 180
NCAND = 64
CHIPQ = 4
PS = 128
HALF = 32
CAP = 16
QUERIES = 64
PASSAGES = 2048
N_SECTION = 2
N_SHARD = 16


def draw_passages(key, part):
    first = jax.random.fold_in(key, 0)
    base = jnp.clip(jax.random.normal(first, (PASSAGES, PLEN, DV), jnp.float32), -6.0, 6.0)
    return base.astype(jnp.bfloat16)


def draw_teacher(key, part):
    first, second = jax.random.split(key)
    offsets = jax.random.uniform(first, (QUERIES, 1), jnp.float32, 0.0, 50.0)
    noise = jnp.clip(jax.random.normal(second, (QUERIES, NCAND), jnp.float32), -6.0, 6.0) * 3.0
    return offsets + noise


def set_ends(drawn, own_key, least, high):
    longest = drawn.shape.index(max(drawn.shape))
    spots = []
    for shift in (0, 1):
        where = [jax.random.randint(jax.random.fold_in(own_key, axis), (), 0, length) for axis, length in enumerate(drawn.shape)]
        where[longest] = (where[longest] + shift) % drawn.shape[longest]
        spots.append(tuple(where))
    return drawn.at[spots[0]].set(least).at[spots[1]].set(high)


def block_levels(key, extent, cuts, low, top_value):
    level = 1.0
    for axis_at, parts in cuts:
        draws = jax.random.uniform(jax.random.fold_in(jax.random.fold_in(key, 6), axis_at), (parts,), jnp.float32, low / len(cuts), top_value / len(cuts))
        level = level * jnp.repeat(jnp.exp(draws), extent[axis_at] // parts).reshape((-1,) + (1,) * (len(extent) - 1 - axis_at))
    return level


def assign_block(own_key, own, number, rows, amount, top, limit, lean):
    ranking = jax.random.permutation(own_key, amount)
    packed, usual = load_shares(amount, rows * top, limit, lean, True), load_shares(amount, rows * top, limit, lean, False)
    places = jnp.arange(amount)

    def named(lengths, turn):
        used = int((lengths > 0).sum())
        fixed = max(1, used // 4)
        shifted = fixed + (places - fixed + turn * (used - fixed)) % max(1, amount - fixed)
        return jnp.zeros((amount,), jnp.int32).at[ranking[jnp.where(places < fixed, places, shifted)]].set(jnp.asarray(lengths, jnp.int32))

    lengths = jnp.where(number % 4 == 0, named(packed, number // 4), named(usual, number - number // 4 - 1))
    mixed = jax.random.permutation(jax.random.fold_in(own, 3), amount)
    source_of, sink = mixed[0:amount // 2 * 2:2], mixed[1:amount // 2 * 2:2]
    room = jnp.minimum(lengths[source_of] - 1, limit - lengths[sink]) // 2
    room = jnp.where((source_of == ranking[0]) | (sink == ranking[0]) | (lengths[sink] == 0), 0, jnp.maximum(room, 0))
    shifted = jax.random.randint(jax.random.fold_in(own, 4), (amount // 2,), 0, 1 << 20) % (room + 1)
    lengths = lengths.at[source_of].add(-shifted).at[sink].add(shifted)
    items = jnp.searchsorted(jnp.cumsum(lengths), jnp.arange(rows * top), side="right").astype(jnp.int32)
    table = items.reshape(top, rows).T
    table = table[jax.random.permutation(jax.random.fold_in(own, 1), rows)]
    turn = jax.random.randint(jax.random.fold_in(own, 2), (rows, 1), 0, top)
    return jnp.take_along_axis(table, (jnp.arange(top)[None, :] + turn) % top, axis=1)


def load_shares(number_of, total, limit, lean, full):
    weights = [(1 << 20) // math.isqrt(standing ** lean) + 1 for standing in range(1, number_of + 1)]
    largest = limit if full else min(limit, max(-(-total // number_of), total * weights[0] // sum(weights)))
    least = 1 if total - largest >= number_of - 1 else 0
    counts, surplus = [largest] + [least] * (number_of - 1), total - largest - least * (number_of - 1)
    while surplus > 0:
        free = [i for i in range(1, number_of) if counts[i] < largest] or [i for i in range(1, number_of) if counts[i] < limit]
        whole, budget = sum([weights[i] for i in free]), surplus
        for i in free:
            more = min(limit - counts[i], max(1, budget * weights[i] // whole), surplus)
            counts[i] = counts[i] + more
            surplus = surplus - more
    return np.array(counts)


def centred(stream_key, shape, scale, reach, pieces=(), kind=jnp.bfloat16):
    loudness = block_levels(stream_key, shape, pieces, -0.22, 0.18) if pieces else 1.0
    entries = jax.random.normal(stream_key, shape, jnp.float32) * scale * loudness
    return jnp.minimum(jnp.maximum(entries, -reach), reach).astype(kind)


def setup_inputs(seed: int = 0) -> dict:
    arg_keys = jax.random.split(jax.random.key(seed), 9)
    hidden = centred(arg_keys[0], (QUERIES, QLEN, D), 1.0, 6.0, ((0, 16), (2, 2)))
    proj = centred(arg_keys[1], (D, DV), D ** -0.5, 0.21875, ((0, 2),))
    passages = draw_passages(jax.random.fold_in(arg_keys[8], 71), 0)
    pass_len = set_ends(jax.random.randint(arg_keys[3], (PASSAGES,), PLEN // 4, PLEN + 1), jax.random.fold_in(arg_keys[3], 1), PLEN // 4, PLEN).astype(jnp.int32)
    query_len = set_ends(jax.random.randint(arg_keys[4], (QUERIES,), QLEN // 4, QLEN + 1), jax.random.fold_in(arg_keys[4], 1), QLEN // 4, QLEN).astype(jnp.int32)
    cand_owner_keys = jax.random.split(jax.random.fold_in(arg_keys[5], 1), N_SECTION * QUERIES * HALF // (CHIPQ * HALF))
    cand_owner_turns = jax.random.permutation(jax.random.fold_in(arg_keys[5], 3), N_SECTION * QUERIES * HALF // (CHIPQ * HALF))
    cand_owner = jax.vmap(lambda own, number: assign_block(jax.random.fold_in(arg_keys[5], 2), own, number, CHIPQ * HALF, N_SHARD, 1, CAP, 2))(cand_owner_keys, cand_owner_turns).reshape((N_SECTION, QUERIES, HALF, 1))
    cand_slot = set_ends(jax.random.randint(arg_keys[6], (N_SECTION, QUERIES, HALF), 0, PS), jax.random.fold_in(arg_keys[6], 1), 0, PS - 1).astype(jnp.int32)
    teacher = draw_teacher(jax.random.fold_in(arg_keys[8], 71), 0)
    return dict(hidden=hidden, proj=proj, passages=passages, pass_len=pass_len, query_len=query_len, cand_owner=cand_owner, cand_slot=cand_slot, teacher=teacher)


SHARPNESS = 64.0
EPSILON = 1e-06
NEGATIVE = -1e+30

def one_query(q_vecs, cand_ids, tok_mask, t_score, passages, pass_len):
    blocks = passages[cand_ids]
    cand_lens = pass_len[cand_ids]
    logits = jnp.einsum('id,ktd->kit', q_vecs.astype(jnp.float32), blocks.astype(jnp.float32)) * SHARPNESS
    in_range = jnp.arange(blocks.shape[1])[None, None, :] < cand_lens[:, None, None]
    logits = jnp.where(in_range, logits, NEGATIVE)
    top_logit = lax.optimization_barrier(jnp.max(logits, axis=2, keepdims=True))
    expo_terms = jnp.where(in_range, jnp.exp(logits - top_logit), 0.0)
    total = lax.optimization_barrier(jnp.sum(expo_terms, axis=2, keepdims=True))
    token_max = (top_logit[..., 0] + jnp.log(total[..., 0])) / SHARPNESS
    token_weight = expo_terms / total
    student = lax.optimization_barrier(jnp.sum(jnp.where(tok_mask[None, :], token_max, 0.0), axis=1))
    teach_top = jnp.max(t_score)
    lse_teach = teach_top + jnp.log(jnp.sum(jnp.exp(t_score - teach_top)))
    stud_top = jnp.max(student)
    lse_stud = stud_top + jnp.log(jnp.sum(jnp.exp(student - stud_top)))
    kl_div = jnp.sum(jnp.exp(t_score - lse_teach) * (t_score - student)) - lse_teach + lse_stud
    score_grad = jnp.exp(student - lse_stud) - jnp.exp(t_score - lse_teach)
    mixed = jnp.where(tok_mask[None, :, None], score_grad[:, None, None] * token_weight, 0.0).astype(jnp.bfloat16)
    vec_grad = jnp.einsum('kit,ktd->id', mixed.astype(jnp.float32), blocks.astype(jnp.float32))
    return (kl_div, vec_grad)

def reference(hidden, proj, passages, pass_len, query_len, cand_owner, cand_slot, teacher):
    num_queries, num_tokens, feat_width = hidden.shape
    vec_dim = proj.shape[1]
    flat_h = hidden.reshape(num_queries * num_tokens, feat_width)
    proj_in = jnp.dot(flat_h, proj, preferred_element_type=jnp.float32).reshape(num_queries, num_tokens, vec_dim)
    inv_norm = lax.rsqrt(lax.optimization_barrier(jnp.sum(proj_in * proj_in, axis=2, keepdims=True)) + EPSILON)
    query_vecs = (proj_in * inv_norm).astype(jnp.bfloat16)
    cand_ids = cand_owner[..., 0] * PS + cand_slot
    cand_ids = jnp.transpose(cand_ids, (1, 0, 2)).reshape(num_queries, NCAND).astype(jnp.int32)
    tok_mask = jnp.arange(num_tokens)[None, :] < query_len[:, None]

    def per_query(inputs_q):
        return one_query(inputs_q[0], inputs_q[1], inputs_q[2], inputs_q[3], passages, pass_len)
    kl_div, vec_grad = lax.map(per_query, (query_vecs, cand_ids, tok_mask, teacher))
    cubed = inv_norm * inv_norm * inv_norm
    in_grad = inv_norm * vec_grad - cubed * proj_in * lax.optimization_barrier(jnp.sum(proj_in * vec_grad, axis=2, keepdims=True))
    flat_in = in_grad.astype(jnp.bfloat16).reshape(num_queries * num_tokens, vec_dim)
    grad_hidden = jnp.dot(flat_in, proj.T, preferred_element_type=jnp.float32).astype(jnp.bfloat16)
    grad_hidden = grad_hidden.reshape(num_queries, num_tokens, feat_width)
    grad_proj = jnp.dot(flat_h.T, flat_in, preferred_element_type=jnp.float32)
    return (kl_div, grad_hidden, grad_proj)
```

```python
import functools
import math

import jax
import jax.numpy as jnp
from jax import lax
from jax.experimental import pallas as pl
from jax.experimental.pallas import tpu as pltpu
from jax.sharding import PartitionSpec as P

SHARPNESS = 64.0
EPSILON = 1e-06
NEGATIVE = -1e30
LANES = 128
GROUP = 4
F32 = jnp.float32
BF16 = jnp.bfloat16
MESH = pl.DeviceIdType.MESH


def iota(shape, axis):
    return lax.broadcasted_iota(jnp.int32, shape, axis)


def remote(src, dst, send, recv, **where):
    return pltpu.make_async_remote_copy(
        src_ref=src, dst_ref=dst, send_sem=send, recv_sem=recv, device_id=where, device_id_type=MESH
    )


def enter(n, me, sec):
    barrier = pltpu.get_barrier_semaphore()
    pl.semaphore_signal(barrier, inc=1, device_id={"section": 1 - sec}, device_id_type=MESH)

    def greet(i, carry):
        pl.semaphore_signal(
            barrier, inc=1, device_id={"shard": lax.rem(me + i, n)}, device_id_type=MESH
        )
        return carry

    lax.fori_loop(1, n, greet, 0)
    pl.semaphore_wait(barrier, n)


def each_peer(n, me, body):
    def step(i, carry):
        body(lax.rem(me + i, n), i)
        return carry

    lax.fori_loop(1, n, step, 0)


def request_kernel(
    n, half_q, nt, h_ref, p_ref, meta_ref,
    q_out, pin_out, tab_out, code_out, info_out,
    part, opart, ometa, tab,
    sib_send, sib_recv, st, rt, sq, rq,
):
    sec, me = lax.axis_index("section"), lax.axis_index("shard")
    rows = half_q * nt
    enter(n, me, sec)
    meta_copy = remote(meta_ref, ometa, sib_send.at[0], sib_recv.at[0], section=1 - sec)
    meta_copy.start()
    part[...] = jnp.dot(h_ref[...], p_ref[...], preferred_element_type=F32)
    other_rows = pl.ds(pl.multiple_of((1 - sec) * rows, rows), rows)
    part_copy = remote(part.at[other_rows], opart, sib_send.at[1], sib_recv.at[1], section=1 - sec)
    part_copy.start()
    meta_copy.wait()

    width = meta_ref.shape[1]
    meta = jnp.concatenate([meta_ref[...], ometa[...]], axis=1)
    owner = meta[0:1, :].astype(jnp.int32)
    code, teach = meta[1:2, :], meta[2:3, :]
    query = meta[3:4, :].astype(jnp.int32)
    valid = (query >= sec * half_q) & (query < (sec + 1) * half_q)
    prob = jnp.zeros_like(teach)
    lane = iota((8, LANES), 1)
    info = jnp.zeros((8, LANES), F32)
    for j in range(half_q):
        mask = query == sec * half_q + j
        top = jnp.max(jnp.where(mask, teach, NEGATIVE), axis=1, keepdims=True)
        terms = jnp.where(mask, jnp.exp(jnp.where(mask, teach - top, 0.0)), 0.0)
        total = jnp.sum(terms, axis=1, keepdims=True)
        prob = prob + terms / total
        info = jnp.where(lane == j, top + jnp.log(total), info)
    info_out[...] = info
    named = jnp.where((iota((n, 2 * width), 0) == owner) & valid, 1.0, 0.0)
    before = jnp.where(iota((2 * width, 2 * width), 0) < iota((2 * width, 2 * width), 1), 1.0, 0.0)
    counts = jnp.dot(named.astype(BF16), before.astype(BF16), preferred_element_type=F32)
    rank = jnp.sum(named * counts, axis=0, keepdims=True).astype(jnp.int32)
    at_rank = jnp.where((iota((LANES, 2 * width), 0) == rank) & valid, 1.0, 0.0)
    line = iota((n * 8, 2 * width), 0)
    kind = line & 7
    value = jnp.where(kind == 0, code, jnp.where(kind == 1, prob, jnp.where(kind == 2, teach, 1.0)))
    value = jnp.where((lax.shift_right_logical(line, 3) == owner) & valid & (kind < 4), value, 0.0)
    table = lax.dot_general(
        value, at_rank, (((1,), (1,)), ((), ())),
        precision=lax.Precision.HIGHEST, preferred_element_type=F32,
    )
    tab[...] = table.reshape(n, 8, LANES)
    each_peer(n, me, lambda p, i: remote(
        tab.at[p], tab_out.at[me], st.at[i], rt.at[me], shard=p).start())
    tab_out[me] = tab[me]

    part_copy.wait()
    pin = part[pl.ds(pl.multiple_of(sec * rows, rows), rows), :] + opart[...]
    pin_out[...] = pin
    inv = lax.rsqrt(jnp.sum(pin * pin, axis=1, keepdims=True) + EPSILON)
    q_out[me] = (pin * inv).astype(BF16)
    each_peer(n, me, lambda p, i: remote(
        q_out.at[me], q_out.at[me], sq.at[i], rq.at[me], shard=p).start())
    each_peer(n, me, lambda p, i: remote(
        tab.at[p], tab_out.at[p], st.at[i], rt.at[p], shard=p).wait())
    got = tab_out[...]
    count = jnp.sum(got[:, 3, :], axis=1, keepdims=True)
    codes = jnp.where(iota((n, LANES), 1) == LANES - 1, count, got[:, 0, :])
    code_out[...] = (codes + 0.5).astype(jnp.int32)
    each_peer(n, me, lambda p, i: remote(
        q_out.at[me], q_out.at[p], sq.at[i], rq.at[p], shard=p).wait())


def score_kernel(
    n, half_q, nt, slot_bits, query_bits, cap,
    code, plen, q_ref, tab_ref, pas_hbm, a_out, t_out, stat_out,
    pas, u_ref, stud_ref, coef_ref, sem,
):
    load = pltpu.make_async_copy(pas_hbm, pas, sem)
    load.start()
    pass_tokens = pas.shape[1]
    scale = SHARPNESS * math.log2(math.e)
    stat_out[...] = jnp.where(iota(stat_out.shape, 0) == 0, NEGATIVE, 0.0)
    load.wait()
    tok = iota((nt, pass_tokens), 1)
    tok_row = iota((nt, 1), 0)

    def per_source(q, carry):
        cnt = code[q, LANES - 1]
        groups = lax.div(cnt + (GROUP - 1), GROUP)

        def group(g, carry):
            for k in range(GROUP):
                r = g * GROUP + k
                c = code[q, r]
                slot = jnp.maximum((c & ((1 << slot_bits) - 1)) - 1, 0)
                which = lax.shift_right_logical(c, slot_bits) & ((1 << query_bits) - 1)
                qlen = lax.shift_right_logical(c, slot_bits + query_bits)
                block = pas[slot]
                vecs = q_ref[q, pl.ds(pl.multiple_of(which * nt, nt), nt), :]
                logits = lax.dot_general(
                    vecs, block, (((1,), (1,)), ((), ())), preferred_element_type=F32
                )
                logits = jnp.where(tok < plen[slot], logits * scale, NEGATIVE)
                top = jnp.max(logits, axis=1, keepdims=True)
                terms = jnp.exp2(logits - top)
                total = jnp.sum(terms, axis=1, keepdims=True)
                best = top * (math.log(2.0) / SHARPNESS) + jnp.log(total) * (1.0 / SHARPNESS)
                student = jnp.sum(jnp.where(tok_row < qlen, best, 0.0), axis=0, keepdims=True)
                unit = jnp.dot(terms.astype(BF16), block, preferred_element_type=F32)
                u_ref[r] = unit * (1.0 / total)
                stud_ref[pl.ds(r, 1), :] = jnp.broadcast_to(student, (1, LANES))
            return carry

        lax.fori_loop(0, groups, group, 0)
        stud = stud_ref[...]
        row_id, lane_id = iota((cap, LANES), 0), iota((cap, LANES), 1)
        table = tab_ref[q]

        def column(v):
            return jnp.sum(
                jnp.where(row_id == lane_id, table[v : v + 1, :], 0.0), axis=1, keepdims=True
            )

        codes = (column(0) + 0.5).astype(jnp.int32)
        prob, teach = column(1), column(2)
        which = lax.shift_right_logical(codes, slot_bits) & ((1 << query_bits) - 1)
        stat = stat_out[...]
        stat_row, stat_lane = iota(stat.shape, 0), iota(stat.shape, 1)
        for j in range(half_q):
            mask = (row_id < cnt) & (which == j)
            top = jnp.max(jnp.where(mask, stud, NEGATIVE), axis=0, keepdims=True)
            terms = jnp.where(mask, jnp.exp(jnp.where(mask, stud - top, 0.0)), 0.0)
            total = jnp.sum(terms, axis=0, keepdims=True)
            cross = jnp.sum(jnp.where(mask, prob * (teach - stud), 0.0), axis=0, keepdims=True)
            coef_ref[j] = terms
            coef_ref[half_q + j] = jnp.where(mask, jnp.broadcast_to(prob, (cap, LANES)), 0.0)
            new = jnp.where(
                stat_row == 0, top[:, :1], jnp.where(stat_row == 1, total[:, :1], cross[:, :1])
            )
            stat = jnp.where((stat_lane == q * half_q + j) & (stat_row < 3), new, stat)
        stat_out[...] = stat

        def gather(g, sums):
            for k in range(GROUP):
                r = g * GROUP + k
                unit = u_ref[r]
                sums = tuple(
                    one + coef_ref[at, pl.ds(r, 1), :] * unit for at, one in enumerate(sums)
                )
            return sums

        zero = jnp.zeros(u_ref.shape[1:], F32)
        sums = lax.fori_loop(0, groups, gather, (zero,) * (2 * half_q))
        for j in range(half_q):
            a_out[q * half_q + j] = sums[j]
            t_out[q * half_q + j] = sums[half_q + j]
        return carry

    lax.fori_loop(0, n, per_source, 0)


def grad_kernel(
    n, half_q, nt, inside, qlen, a_ref, t_ref, stat_ref, pin_ref, info_ref, h_ref, p_ref,
    kl_out, gh_out, gp_out,
    stats, crow, psend, rpart, ing, klbuf, lp, rs,
    sib_send, sib_recv, s0, r0, s1, r1, s2, r2, s3, r3,
):
    sec, me = lax.axis_index("section"), lax.axis_index("shard")
    rows = half_q * nt
    width = stat_ref.shape[1]
    enter(n, me, sec)
    each_peer(n, me, lambda p, i: remote(
        stat_ref, stats.at[me], s0.at[i], r0.at[me], shard=p).start())
    stats[me] = stat_ref[...]
    each_peer(n, me, lambda p, i: remote(
        stat_ref, stats.at[p], s0.at[i], r0.at[p], shard=p).wait())
    tops, totals, crosses = stats[:, 0, :], stats[:, 1, :], stats[:, 2, :]
    top = jnp.max(tops, axis=0, keepdims=True)
    lse = top + jnp.log(jnp.sum(totals * jnp.exp(tops - top), axis=0, keepdims=True))
    cross = jnp.sum(crosses, axis=0, keepdims=True)
    factor = jnp.exp(stat_ref[0:1, :] - lse)
    count = crow.shape[0]
    crow[...] = jnp.broadcast_to(
        jnp.sum(
            jnp.where(iota((count, width), 0) == iota((count, width), 1), factor, 0.0),
            axis=1, keepdims=True,
        ),
        crow.shape,
    )

    def make_part(p):
        for j in range(half_q):
            at = p * half_q + j
            value = a_ref[at] * crow[pl.ds(at, 1), :] - t_ref[at]
            psend[p, j * nt : (j + 1) * nt, :] = value.astype(BF16)

    def send_part(p, i):
        make_part(p)
        remote(psend.at[p], rpart.at[me], s1.at[i], r1.at[me], shard=p).start()

    each_peer(n, me, send_part)
    make_part(me)
    rpart[me] = psend[me]

    kl = jnp.zeros((8, LANES), F32)
    lane = iota((1, width), 1)
    for j in range(half_q):
        mine = jnp.sum(jnp.where(lane == me * half_q + j, cross + lse, 0.0), axis=1, keepdims=True)
        kl = jnp.where(
            iota((8, LANES), 1) == sec * half_q + j, mine - info_ref[0:1, j : j + 1], kl
        )
    klbuf[sec] = kl
    kl_copy = remote(klbuf.at[sec], klbuf.at[sec], sib_send.at[0], sib_recv.at[0], section=1 - sec)
    kl_copy.start()
    pin = pin_ref[...]
    inv = lax.rsqrt(jnp.sum(pin * pin, axis=1, keepdims=True) + EPSILON)

    each_peer(n, me, lambda p, i: remote(
        psend.at[p], rpart.at[p], s1.at[i], r1.at[p], shard=p).wait())
    vec = lax.fori_loop(
        0, n, lambda o, total: total + rpart[o].astype(F32), jnp.zeros((rows, LANES), F32)
    )
    tok = iota((nt, LANES), 0)
    vec = jnp.concatenate(
        [
            jnp.where(tok < qlen[sec * half_q + j], vec[j * nt : (j + 1) * nt, :], 0.0)
            for j in range(half_q)
        ],
        axis=0,
    )
    grad = inv * vec - inv * inv * inv * pin * jnp.sum(pin * vec, axis=1, keepdims=True)
    own = pl.ds(pl.multiple_of(sec * rows, rows), rows)
    ing[own, :] = grad.astype(BF16)
    in_copy = remote(ing.at[own], ing.at[own], sib_send.at[1], sib_recv.at[1], section=1 - sec)
    in_copy.start()
    kl_copy.wait()
    kl_out[...] = klbuf[0] + klbuf[1]
    in_copy.wait()
    flat = ing[...]
    terms = lax.dot_general(
        h_ref[...], flat, (((0,), (0,)), ((), ())), preferred_element_type=F32
    )
    if inside:
        lp[...] = terms
        piece = terms.shape[0] // n

        def span(p):
            return pl.ds(pl.multiple_of(p * piece, 8), piece)

        each_peer(n, me, lambda p, i: remote(
            lp.at[span(p)], rs.at[me], s2.at[i], r2.at[me], shard=p).start())
        rs[me] = lp[span(me), :]
    else:
        gp_out[...] = terms
    gh_out[...] = lax.dot_general(
        flat, p_ref[...], (((1,), (1,)), ((), ())), preferred_element_type=F32
    ).astype(BF16)
    if inside:
        each_peer(n, me, lambda p, i: remote(
            lp.at[span(p)], rs.at[p], s2.at[i], r2.at[p], shard=p).wait())
        gp_out[span(me), :] = jnp.sum(rs[...], axis=0)
        each_peer(n, me, lambda p, i: remote(
            gp_out.at[span(me)], gp_out.at[span(me)], s3.at[i], r3.at[me], shard=p).start())
        each_peer(n, me, lambda p, i: remote(
            gp_out.at[span(me)], gp_out.at[span(p)], s3.at[i], r3.at[p], shard=p).wait())


def local(hidden, proj, passages, pass_len, query_len, cand_owner, cand_slot, teacher):
    nq, nt, feat = hidden.shape
    dv = proj.shape[1]
    slots, pass_tokens, _ = passages.shape
    n = lax.axis_size("shard")
    half_q = nq // 2
    rows = half_q * nt
    requests = cand_owner.size
    cap = max(8, 2 * max(2, (2 * requests + n - 1) // n))
    slot_bits = slots.bit_length()
    query_bits = max(1, (half_q - 1).bit_length())
    width = -(-(n * half_q) // LANES) * LANES
    flat_h = hidden.reshape(nq * nt, feat)

    query = jnp.broadcast_to(jnp.arange(nq)[:, None], teacher.shape)
    code = (
        cand_slot.reshape(teacher.shape)
        + 1
        + ((query % half_q) << slot_bits)
        + (query_len[:, None] << (slot_bits + query_bits))
    )
    zero = jnp.zeros((requests,), F32)
    meta = jnp.stack(
        [
            cand_owner.reshape(-1).astype(F32),
            code.reshape(-1).astype(F32),
            teacher.reshape(-1),
            query.reshape(-1).astype(F32),
            zero, zero, zero, zero,
        ]
    )
    vmem = pl.BlockSpec(memory_space=pltpu.VMEM)
    smem = pl.BlockSpec(memory_space=pltpu.SMEM)
    dma = pltpu.SemaphoreType.DMA
    shape = jax.ShapeDtypeStruct
    q_all, pin, tab, codes, info = pl.pallas_call(
        functools.partial(request_kernel, n, half_q, nt),
        out_shape=(
            shape((n, rows, dv), BF16),
            shape((rows, dv), F32),
            shape((n, 8, LANES), F32),
            shape((n, LANES), jnp.int32),
            shape((8, LANES), F32),
        ),
        in_specs=[vmem] * 3,
        out_specs=(vmem,) * 5,
        scratch_shapes=[
            pltpu.VMEM((nq * nt, dv), F32),
            pltpu.VMEM((rows, dv), F32),
            pltpu.VMEM((8, requests), F32),
            pltpu.VMEM((n, 8, LANES), F32),
            dma((2,)), dma((2,)), dma((n,)), dma((n,)), dma((n,)), dma((n,)),
        ],
        compiler_params=pltpu.CompilerParams(
            collective_id=0, has_side_effects=True, vmem_limit_bytes=32 << 20
        ),
        name="requests",
    )(flat_h, proj, meta)

    a_part, t_part, stat = pl.pallas_call(
        functools.partial(score_kernel, n, half_q, nt, slot_bits, query_bits, cap),
        out_shape=(
            shape((n * half_q, nt, dv), F32),
            shape((n * half_q, nt, dv), F32),
            shape((8, width), F32),
        ),
        in_specs=[smem, smem, vmem, vmem, pl.BlockSpec(memory_space=pl.ANY)],
        out_specs=(vmem,) * 3,
        scratch_shapes=[
            pltpu.VMEM((slots, pass_tokens, dv), BF16),
            pltpu.VMEM((cap, nt, dv), F32),
            pltpu.VMEM((cap, LANES), F32),
            pltpu.VMEM((2 * half_q, cap, LANES), F32),
            dma,
        ],
        compiler_params=pltpu.CompilerParams(vmem_limit_bytes=48 << 20),
        name="scores",
    )(codes, pass_len, q_all, tab, passages)

    inside = feat % n == 0 and (feat // n) % 8 == 0
    piece = feat // n if inside else 8
    kl, gh, gp = pl.pallas_call(
        functools.partial(grad_kernel, n, half_q, nt, inside),
        out_shape=(
            shape((8, LANES), F32),
            shape((nq * nt, feat), BF16),
            shape((feat, dv), F32),
        ),
        in_specs=[smem] + [vmem] * 7,
        out_specs=(vmem,) * 3,
        scratch_shapes=[
            pltpu.VMEM((n, 8, width), F32),
            pltpu.VMEM((n * half_q, LANES), F32),
            pltpu.VMEM((n, rows, dv), BF16),
            pltpu.VMEM((n, rows, dv), BF16),
            pltpu.VMEM((nq * nt, dv), BF16),
            pltpu.VMEM((2, 8, LANES), F32),
            pltpu.VMEM((feat, dv), F32),
            pltpu.VMEM((n, piece, dv), F32),
            dma((2,)), dma((2,)),
        ]
        + [dma((n,))] * 8,
        compiler_params=pltpu.CompilerParams(
            collective_id=1, has_side_effects=True, vmem_limit_bytes=48 << 20
        ),
        name="grads",
    )(query_len, a_part, t_part, stat, pin, info, flat_h, proj)
    if not inside:
        gp = lax.psum(gp, "shard")
    return kl[0, :nq], gh.reshape(nq, nt, feat), gp


def solution(mesh):
    in_specs = (
        P("shard", None, "section"),
        P("section", None),
        P("shard", None, None),
        P("shard"),
        P("shard"),
        P("section", "shard", None, None),
        P("section", "shard", None),
        P("shard", "section"),
    )
    out_specs = (P("shard"), P("shard", None, "section"), P("section", None))
    return jax.shard_map(local, mesh=mesh, in_specs=in_specs, out_specs=out_specs, check_vma=False)
```

```python
import functools
import math

import jax
import jax.numpy as jnp
from jax import lax
from jax.experimental import pallas as pl
from jax.experimental.pallas import tpu as pltpu
from jax.sharding import PartitionSpec as P

SHARPNESS = 64.0
EPSILON = 1e-06
NEGATIVE = -1e30
LANES = 128
GROUP = 8
CHUNK = 64
F32 = jnp.float32
BF16 = jnp.bfloat16
MESH = pl.DeviceIdType.MESH


def iota(shape, axis):
    return lax.broadcasted_iota(jnp.int32, shape, axis)


def remote(src, dst, send, recv, **where):
    return pltpu.make_async_remote_copy(
        src_ref=src, dst_ref=dst, send_sem=send, recv_sem=recv, device_id=where, device_id_type=MESH
    )


def enter(n, me, sec):
    barrier = pltpu.get_barrier_semaphore()
    pl.semaphore_signal(barrier, inc=1, device_id={"section": 1 - sec}, device_id_type=MESH)

    def greet(i, carry):
        pl.semaphore_signal(
            barrier, inc=1, device_id={"shard": lax.rem(me + i, n)}, device_id_type=MESH
        )
        return carry

    lax.fori_loop(1, n, greet, 0)
    pl.semaphore_wait(barrier, n)


def each_peer(n, me, body):
    def step(i, carry):
        body(lax.rem(me + i, n), i)
        return carry

    lax.fori_loop(1, n, step, 0)


def request_kernel(
    n, half_q, nt, h_ref, p_ref, meta_ref,
    q_out, pin_out, code_out, prob_out, teach_out, info_out,
    tab_out, part, opart, ometa, tab,
    sib_send, sib_recv, st, rt, sq, rq,
):
    sec, me = lax.axis_index("section"), lax.axis_index("shard")
    rows = half_q * nt
    enter(n, me, sec)
    meta_copy = remote(meta_ref, ometa, sib_send.at[0], sib_recv.at[0], section=1 - sec)
    meta_copy.start()
    part[...] = jnp.dot(h_ref[...], p_ref[...], preferred_element_type=F32)
    other_rows = pl.ds(pl.multiple_of((1 - sec) * rows, rows), rows)
    part_copy = remote(part.at[other_rows], opart, sib_send.at[1], sib_recv.at[1], section=1 - sec)
    part_copy.start()
    meta_copy.wait()

    width = meta_ref.shape[1]
    meta = jnp.concatenate([meta_ref[...], ometa[...]], axis=1)
    owner = meta[0:1, :].astype(jnp.int32)
    code, teach = meta[1:2, :], meta[2:3, :]
    query = meta[3:4, :].astype(jnp.int32)
    valid = (query >= sec * half_q) & (query < (sec + 1) * half_q)
    prob = jnp.zeros_like(teach)
    lane = iota((8, LANES), 1)
    info = jnp.zeros((8, LANES), F32)
    for j in range(half_q):
        mask = query == sec * half_q + j
        top = jnp.max(jnp.where(mask, teach, NEGATIVE), axis=1, keepdims=True)
        terms = jnp.where(mask, jnp.exp(jnp.where(mask, teach - top, 0.0)), 0.0)
        total = jnp.sum(terms, axis=1, keepdims=True)
        prob = prob + terms / total
        info = jnp.where(lane == j, top + jnp.log(total), info)
    info_out[...] = info
    named = jnp.where((iota((n, 2 * width), 0) == owner) & valid, 1.0, 0.0)
    before = jnp.where(iota((2 * width, 2 * width), 0) < iota((2 * width, 2 * width), 1), 1.0, 0.0)
    counts = jnp.dot(named.astype(BF16), before.astype(BF16), preferred_element_type=F32)
    rank = jnp.sum(named * counts, axis=0, keepdims=True).astype(jnp.int32)
    at_rank = jnp.where((iota((LANES, 2 * width), 0) == rank) & valid, 1.0, 0.0)
    line = iota((n * 8, 2 * width), 0)
    kind = line & 7
    value = jnp.where(kind == 0, code, jnp.where(kind == 1, prob, jnp.where(kind == 2, teach, 1.0)))
    value = jnp.where((lax.shift_right_logical(line, 3) == owner) & valid & (kind < 4), value, 0.0)
    table = lax.dot_general(
        value, at_rank, (((1,), (1,)), ((), ())),
        precision=lax.Precision.HIGHEST, preferred_element_type=F32,
    )
    tab[...] = table.reshape(n, 8, LANES)
    each_peer(n, me, lambda p, i: remote(
        tab.at[p], tab_out.at[me], st.at[i], rt.at[me], shard=p).start())
    tab_out[me] = tab[me]

    part_copy.wait()
    pin = part[pl.ds(pl.multiple_of(sec * rows, rows), rows), :] + opart[...]
    pin_out[...] = pin
    inv = lax.rsqrt(jnp.sum(pin * pin, axis=1, keepdims=True) + EPSILON)
    q_out[me] = (pin * inv).astype(BF16)
    each_peer(n, me, lambda p, i: remote(
        q_out.at[me], q_out.at[me], sq.at[i], rq.at[me], shard=p).start())
    each_peer(n, me, lambda p, i: remote(
        tab.at[p], tab_out.at[p], st.at[i], rt.at[p], shard=p).wait())
    got = tab_out[...]
    count = jnp.sum(got[:, 3, :], axis=1, keepdims=True)
    codes = jnp.where(iota((n, LANES), 1) == LANES - 1, count, got[:, 0, :])
    code_out[...] = (codes + 0.5).astype(jnp.int32)
    prob_out[...] = got[:, 1, :]
    teach_out[...] = got[:, 2, :]
    each_peer(n, me, lambda p, i: remote(
        q_out.at[me], q_out.at[p], sq.at[i], rq.at[p], shard=p).wait())


def score_kernel(
    n, half_q, nt, slot_bits, query_bits,
    code, prob, teach, plen, q_ref, pas_hbm, a_out, t_out, stat_out,
    pas, u_ref, stud_ref, own_ref, prob_ref, teach_ref, coef_ref, listing, sem,
):
    load = pltpu.make_async_copy(pas_hbm, pas, sem)
    load.start()
    pass_tokens = pas.shape[1]
    scale = SHARPNESS * math.log2(math.e)
    len_bits = nt.bit_length()
    high = slot_bits + query_bits + len_bits

    def per_source(q, start):
        cnt = code[q, LANES - 1]

        def eight(g, carry):
            for k in range(8):
                r = g * 8 + k
                e = start + r
                listing[e] = code[q, r] | lax.shift_left(q, high)
                prob_ref[pl.ds(e, 1), :] = jnp.full((1, LANES), prob[q, r], F32)
                teach_ref[pl.ds(e, 1), :] = jnp.full((1, LANES), teach[q, r], F32)
            return carry

        lax.fori_loop(0, lax.shift_right_logical(cnt + 7, 3), eight, 0)
        return start + cnt

    count = lax.fori_loop(0, n, per_source, 0)
    for k in range(GROUP):
        listing[count + k] = 0
    groups = lax.div(count + (GROUP - 1), GROUP)
    tok = iota((nt, pass_tokens), 1)
    tok_row = iota((nt, 1), 0)

    def place(c):
        which = lax.shift_right_logical(c, slot_bits) & ((1 << query_bits) - 1)
        return lax.shift_right_logical(c, high), which

    load.wait()

    def group(g, carry):
        for k in range(GROUP):
            e = g * GROUP + k
            c = listing[e]
            slot = jnp.maximum((c & ((1 << slot_bits) - 1)) - 1, 0)
            q, which = place(c)
            qlen = lax.shift_right_logical(c, slot_bits + query_bits) & ((1 << len_bits) - 1)
            block = pas[slot]
            vecs = q_ref[q, pl.ds(pl.multiple_of(which * nt, nt), nt), :]
            logits = lax.dot_general(
                vecs, block, (((1,), (1,)), ((), ())), preferred_element_type=F32
            )
            logits = jnp.where(tok < plen[slot], logits * scale, NEGATIVE)
            top = jnp.max(logits, axis=1, keepdims=True)
            terms = jnp.exp2(logits - top)
            total = jnp.sum(terms, axis=1, keepdims=True)
            best = top * (math.log(2.0) / SHARPNESS) + jnp.log(total) * (1.0 / SHARPNESS)
            student = jnp.sum(jnp.where(tok_row < qlen, best, 0.0), axis=0, keepdims=True)
            unit = jnp.dot(terms.astype(BF16), block, preferred_element_type=F32)
            u_ref[e] = unit * (1.0 / total)
            stud_ref[pl.ds(e, 1), :] = jnp.broadcast_to(student, (1, LANES))
            own_ref[pl.ds(e, 1), :] = jnp.full((1, LANES), q * half_q + which, jnp.int32)
        return carry

    lax.fori_loop(0, groups, group, 0)

    width = stat_out.shape[1]
    chunks = lax.div(count + (CHUNK - 1), CHUNK)

    def wide(x):
        return x if width == LANES else jnp.concatenate([x] * (width // LANES), axis=1)

    def chunk(c):
        at = pl.ds(pl.multiple_of(c * CHUNK, CHUNK), CHUNK)
        valid = iota((CHUNK, 1), 0) + c * CHUNK < count
        mask = (wide(own_ref[at, :]) == iota((CHUNK, width), 1)) & valid
        return at, valid, mask, stud_ref[at, :]

    def find_top(c, top):
        at, valid, mask, stud = chunk(c)
        return jnp.maximum(
            top, jnp.max(jnp.where(mask, wide(stud), NEGATIVE), axis=0, keepdims=True)
        )

    none = jnp.zeros((1, width), F32)
    top = lax.fori_loop(0, chunks, find_top, none + NEGATIVE)

    def weigh(c, sums):
        at, valid, mask, stud = chunk(c)
        mine = jnp.max(jnp.where(mask, top, NEGATIVE), axis=1, keepdims=True)
        terms = jnp.where(valid, jnp.exp(jnp.where(valid, stud - mine, 0.0)), 0.0)
        likely = jnp.where(valid, prob_ref[at, :], 0.0)
        coef_ref[at, :] = terms
        cross = jnp.where(valid, likely * (teach_ref[at, :] - stud), 0.0)
        prob_ref[at, :] = likely
        return (
            sums[0] + jnp.sum(jnp.where(mask, wide(terms), 0.0), axis=0, keepdims=True),
            sums[1] + jnp.sum(jnp.where(mask, wide(cross), 0.0), axis=0, keepdims=True),
        )

    total, cross = lax.fori_loop(0, chunks, weigh, (none, none))
    stat_out[...] = jnp.concatenate([top, total, cross, jnp.zeros((5, width), F32)], axis=0)
    a_out[...] = jnp.zeros_like(a_out)
    t_out[...] = jnp.zeros_like(t_out)

    def gather(g, carry):
        for k in range(4):
            e = g * 4 + k
            q, which = place(listing[e])
            at = q * half_q + which
            unit = u_ref[e]
            a_out[at] += coef_ref[pl.ds(e, 1), :] * unit
            t_out[at] += prob_ref[pl.ds(e, 1), :] * unit
        return carry

    lax.fori_loop(0, lax.shift_right_logical(count + 3, 2), gather, 0)


def grad_kernel(
    n, half_q, nt, inside, qlen, a_ref, t_ref, stat_ref, pin_ref, info_ref, h_ref, p_ref,
    kl_out, gh_out, gp_out,
    stats, crow, psend, rpart, ing, klbuf, lp, rs,
    sib_send, sib_recv, s0, r0, s1, r1, s2, r2, s3, r3,
):
    sec, me = lax.axis_index("section"), lax.axis_index("shard")
    rows = half_q * nt
    width = stat_ref.shape[1]
    enter(n, me, sec)
    each_peer(n, me, lambda p, i: remote(
        stat_ref, stats.at[me], s0.at[i], r0.at[me], shard=p).start())
    stats[me] = stat_ref[...]
    each_peer(n, me, lambda p, i: remote(
        stat_ref, stats.at[p], s0.at[i], r0.at[p], shard=p).wait())
    tops, totals, crosses = stats[:, 0, :], stats[:, 1, :], stats[:, 2, :]
    top = jnp.max(tops, axis=0, keepdims=True)
    lse = top + jnp.log(jnp.sum(totals * jnp.exp(tops - top), axis=0, keepdims=True))
    cross = jnp.sum(crosses, axis=0, keepdims=True)
    factor = jnp.exp(stat_ref[0:1, :] - lse)
    count = crow.shape[0]
    crow[...] = jnp.broadcast_to(
        jnp.sum(
            jnp.where(iota((count, width), 0) == iota((count, width), 1), factor, 0.0),
            axis=1, keepdims=True,
        ),
        crow.shape,
    )

    def make_part(p):
        for j in range(half_q):
            at = p * half_q + j
            value = a_ref[at] * crow[pl.ds(at, 1), :] - t_ref[at]
            psend[p, j * nt : (j + 1) * nt, :] = value.astype(BF16)

    def send_part(p, i):
        make_part(p)
        remote(psend.at[p], rpart.at[me], s1.at[i], r1.at[me], shard=p).start()

    each_peer(n, me, send_part)
    make_part(me)
    rpart[me] = psend[me]

    kl = jnp.zeros((8, LANES), F32)
    lane = iota((1, width), 1)
    for j in range(half_q):
        mine = jnp.sum(jnp.where(lane == me * half_q + j, cross + lse, 0.0), axis=1, keepdims=True)
        kl = jnp.where(
            iota((8, LANES), 1) == sec * half_q + j, mine - info_ref[0:1, j : j + 1], kl
        )
    klbuf[sec] = kl
    kl_copy = remote(klbuf.at[sec], klbuf.at[sec], sib_send.at[0], sib_recv.at[0], section=1 - sec)
    kl_copy.start()
    pin = pin_ref[...]
    inv = lax.rsqrt(jnp.sum(pin * pin, axis=1, keepdims=True) + EPSILON)

    each_peer(n, me, lambda p, i: remote(
        psend.at[p], rpart.at[p], s1.at[i], r1.at[p], shard=p).wait())
    vec = lax.fori_loop(
        0, n, lambda o, total: total + rpart[o].astype(F32), jnp.zeros((rows, LANES), F32)
    )
    tok = iota((nt, LANES), 0)
    vec = jnp.concatenate(
        [
            jnp.where(tok < qlen[sec * half_q + j], vec[j * nt : (j + 1) * nt, :], 0.0)
            for j in range(half_q)
        ],
        axis=0,
    )
    grad = inv * vec - inv * inv * inv * pin * jnp.sum(pin * vec, axis=1, keepdims=True)
    own = pl.ds(pl.multiple_of(sec * rows, rows), rows)
    ing[own, :] = grad.astype(BF16)
    in_copy = remote(ing.at[own], ing.at[own], sib_send.at[1], sib_recv.at[1], section=1 - sec)
    in_copy.start()
    kl_copy.wait()
    kl_out[...] = klbuf[0] + klbuf[1]
    in_copy.wait()
    flat = ing[...]
    terms = lax.dot_general(
        h_ref[...], flat, (((0,), (0,)), ((), ())), preferred_element_type=F32
    )
    if inside:
        lp[...] = terms
        piece = terms.shape[0] // n

        def span(p):
            return pl.ds(pl.multiple_of(p * piece, 8), piece)

        each_peer(n, me, lambda p, i: remote(
            lp.at[span(p)], rs.at[me], s2.at[i], r2.at[me], shard=p).start())
        rs[me] = lp[span(me), :]
    else:
        gp_out[...] = terms
    gh_out[...] = lax.dot_general(
        flat, p_ref[...], (((1,), (1,)), ((), ())), preferred_element_type=F32
    ).astype(BF16)
    if inside:
        each_peer(n, me, lambda p, i: remote(
            lp.at[span(p)], rs.at[p], s2.at[i], r2.at[p], shard=p).wait())
        gp_out[span(me), :] = jnp.sum(rs[...], axis=0)
        each_peer(n, me, lambda p, i: remote(
            gp_out.at[span(me)], gp_out.at[span(me)], s3.at[i], r3.at[me], shard=p).start())
        each_peer(n, me, lambda p, i: remote(
            gp_out.at[span(me)], gp_out.at[span(p)], s3.at[i], r3.at[p], shard=p).wait())


def local(hidden, proj, passages, pass_len, query_len, cand_owner, cand_slot, teacher):
    nq, nt, feat = hidden.shape
    dv = proj.shape[1]
    slots, pass_tokens, _ = passages.shape
    n = lax.axis_size("shard")
    half_q = nq // 2
    rows = half_q * nt
    requests = cand_owner.size
    cap = 2 * max(2, (2 * requests + n - 1) // n)
    most = -(-(n * cap + 8) // CHUNK) * CHUNK
    slot_bits = slots.bit_length()
    query_bits = max(1, (half_q - 1).bit_length())
    width = -(-(n * half_q) // LANES) * LANES
    flat_h = hidden.reshape(nq * nt, feat)

    query = jnp.broadcast_to(jnp.arange(nq)[:, None], teacher.shape)
    code = (
        cand_slot.reshape(teacher.shape)
        + 1
        + ((query % half_q) << slot_bits)
        + (query_len[:, None] << (slot_bits + query_bits))
    )
    zero = jnp.zeros((requests,), F32)
    meta = jnp.stack(
        [
            cand_owner.reshape(-1).astype(F32),
            code.reshape(-1).astype(F32),
            teacher.reshape(-1),
            query.reshape(-1).astype(F32),
            zero, zero, zero, zero,
        ]
    )
    vmem = pl.BlockSpec(memory_space=pltpu.VMEM)
    smem = pl.BlockSpec(memory_space=pltpu.SMEM)
    dma = pltpu.SemaphoreType.DMA
    shape = jax.ShapeDtypeStruct
    q_all, pin, codes, probs, teachs, info = pl.pallas_call(
        functools.partial(request_kernel, n, half_q, nt),
        out_shape=(
            shape((n, rows, dv), BF16),
            shape((rows, dv), F32),
            shape((n, LANES), jnp.int32),
            shape((n, LANES), F32),
            shape((n, LANES), F32),
            shape((8, LANES), F32),
        ),
        in_specs=[vmem] * 3,
        out_specs=(vmem,) * 6,
        scratch_shapes=[
            pltpu.VMEM((n, 8, LANES), F32),
            pltpu.VMEM((nq * nt, dv), F32),
            pltpu.VMEM((rows, dv), F32),
            pltpu.VMEM((8, requests), F32),
            pltpu.VMEM((n, 8, LANES), F32),
            dma((2,)), dma((2,)), dma((n,)), dma((n,)), dma((n,)), dma((n,)),
        ],
        compiler_params=pltpu.CompilerParams(
            collective_id=0, has_side_effects=True, vmem_limit_bytes=32 << 20
        ),
        name="requests",
    )(flat_h, proj, meta)

    a_part, t_part, stat = pl.pallas_call(
        functools.partial(score_kernel, n, half_q, nt, slot_bits, query_bits),
        out_shape=(
            shape((n * half_q, nt, dv), F32),
            shape((n * half_q, nt, dv), F32),
            shape((8, width), F32),
        ),
        in_specs=[smem] * 4 + [vmem, pl.BlockSpec(memory_space=pl.ANY)],
        out_specs=(vmem,) * 3,
        scratch_shapes=[
            pltpu.VMEM((slots, pass_tokens, dv), BF16),
            pltpu.VMEM((most, nt, dv), F32),
            pltpu.VMEM((most, LANES), F32),
            pltpu.VMEM((most, LANES), jnp.int32),
            pltpu.VMEM((most, LANES), F32),
            pltpu.VMEM((most, LANES), F32),
            pltpu.VMEM((most, LANES), F32),
            pltpu.SMEM((most,), jnp.int32),
            dma,
        ],
        compiler_params=pltpu.CompilerParams(vmem_limit_bytes=48 << 20),
        name="scores",
    )(codes, probs, teachs, pass_len, q_all, passages)

    inside = feat % n == 0 and (feat // n) % 8 == 0
    piece = feat // n if inside else 8
    kl, gh, gp = pl.pallas_call(
        functools.partial(grad_kernel, n, half_q, nt, inside),
        out_shape=(
            shape((8, LANES), F32),
            shape((nq * nt, feat), BF16),
            shape((feat, dv), F32),
        ),
        in_specs=[smem] + [vmem] * 7,
        out_specs=(vmem,) * 3,
        scratch_shapes=[
            pltpu.VMEM((n, 8, width), F32),
            pltpu.VMEM((n * half_q, LANES), F32),
            pltpu.VMEM((n, rows, dv), BF16),
            pltpu.VMEM((n, rows, dv), BF16),
            pltpu.VMEM((nq * nt, dv), BF16),
            pltpu.VMEM((2, 8, LANES), F32),
            pltpu.VMEM((feat, dv), F32),
            pltpu.VMEM((n, piece, dv), F32),
            dma((2,)), dma((2,)),
        ]
        + [dma((n,))] * 8,
        compiler_params=pltpu.CompilerParams(
            collective_id=1, has_side_effects=True, vmem_limit_bytes=48 << 20
        ),
        name="grads",
    )(query_len, a_part, t_part, stat, pin, info, flat_h, proj)
    if not inside:
        gp = lax.psum(gp, "shard")
    return kl[0, :nq], gh.reshape(nq, nt, feat), gp


def solution(mesh):
    in_specs = (
        P("shard", None, "section"),
        P("section", None),
        P("shard", None, None),
        P("shard"),
        P("shard"),
        P("section", "shard", None, None),
        P("section", "shard", None),
        P("shard", "section"),
    )
    out_specs = (P("shard"), P("shard", None, "section"), P("section", None))
    return jax.shard_map(local, mesh=mesh, in_specs=in_specs, out_specs=out_specs, check_vma=False)
```

```python
import functools
import math

import jax
import jax.numpy as jnp
from jax import lax
from jax.experimental import pallas as pl
from jax.experimental.pallas import tpu as pltpu
from jax.sharding import PartitionSpec as P

SHARPNESS = 64.0
EPSILON = 1e-06
NEGATIVE = -1e30
LANES = 128
GROUP = 8
CHUNK = 64
F32 = jnp.float32
BF16 = jnp.bfloat16
MESH = pl.DeviceIdType.MESH


def iota(shape, axis):
    return lax.broadcasted_iota(jnp.int32, shape, axis)


def remote(src, dst, send, recv, **where):
    return pltpu.make_async_remote_copy(
        src_ref=src, dst_ref=dst, send_sem=send, recv_sem=recv, device_id=where, device_id_type=MESH
    )


def enter(n, me, sec):
    barrier = pltpu.get_barrier_semaphore()
    pl.semaphore_signal(barrier, inc=1, device_id={"section": 1 - sec}, device_id_type=MESH)

    def greet(i, carry):
        pl.semaphore_signal(
            barrier, inc=1, device_id={"shard": lax.rem(me + i, n)}, device_id_type=MESH
        )
        return carry

    lax.fori_loop(1, n, greet, 0)
    pl.semaphore_wait(barrier, n)


def each_peer(n, me, body):
    def step(i, carry):
        body(lax.rem(me + i, n), i)
        return carry

    lax.fori_loop(1, n, step, 0)


def request_kernel(
    n, half_q, nt, h_ref, p_ref, meta_ref,
    q_out, pin_out, code_out, prob_out, teach_out, info_out,
    tab_out, part, opart, ometa, tab,
    sib_send, sib_recv, st, rt, sq, rq,
):
    sec, me = lax.axis_index("section"), lax.axis_index("shard")
    rows = half_q * nt
    enter(n, me, sec)
    meta_copy = remote(meta_ref, ometa, sib_send.at[0], sib_recv.at[0], section=1 - sec)
    meta_copy.start()
    part[...] = jnp.dot(h_ref[...], p_ref[...], preferred_element_type=F32)
    other_rows = pl.ds(pl.multiple_of((1 - sec) * rows, rows), rows)
    part_copy = remote(part.at[other_rows], opart, sib_send.at[1], sib_recv.at[1], section=1 - sec)
    part_copy.start()
    meta_copy.wait()

    width = meta_ref.shape[1]
    meta = jnp.concatenate([meta_ref[...], ometa[...]], axis=1)
    owner = meta[0:1, :].astype(jnp.int32)
    code, teach = meta[1:2, :], meta[2:3, :]
    query = meta[3:4, :].astype(jnp.int32)
    valid = (query >= sec * half_q) & (query < (sec + 1) * half_q)
    prob = jnp.zeros_like(teach)
    lane = iota((8, LANES), 1)
    info = jnp.zeros((8, LANES), F32)
    for j in range(half_q):
        mask = query == sec * half_q + j
        top = jnp.max(jnp.where(mask, teach, NEGATIVE), axis=1, keepdims=True)
        terms = jnp.where(mask, jnp.exp(jnp.where(mask, teach - top, 0.0)), 0.0)
        total = jnp.sum(terms, axis=1, keepdims=True)
        prob = prob + terms / total
        info = jnp.where(lane == j, top + jnp.log(total), info)
    info_out[...] = info
    named = jnp.where((iota((n, 2 * width), 0) == owner) & valid, 1.0, 0.0)
    before = jnp.where(iota((2 * width, 2 * width), 0) < iota((2 * width, 2 * width), 1), 1.0, 0.0)
    counts = jnp.dot(named.astype(BF16), before.astype(BF16), preferred_element_type=F32)
    rank = jnp.sum(named * counts, axis=0, keepdims=True).astype(jnp.int32)
    at_rank = jnp.where((iota((LANES, 2 * width), 0) == rank) & valid, 1.0, 0.0)
    line = iota((n * 8, 2 * width), 0)
    kind = line & 7
    value = jnp.where(kind == 0, code, jnp.where(kind == 1, prob, jnp.where(kind == 2, teach, 1.0)))
    value = jnp.where((lax.shift_right_logical(line, 3) == owner) & valid & (kind < 4), value, 0.0)
    table = lax.dot_general(
        value, at_rank, (((1,), (1,)), ((), ())),
        precision=lax.Precision.HIGHEST, preferred_element_type=F32,
    )
    tab[...] = table.reshape(n, 8, LANES)
    each_peer(n, me, lambda p, i: remote(
        tab.at[p], tab_out.at[me], st.at[i], rt.at[me], shard=p).start())
    tab_out[me] = tab[me]

    part_copy.wait()
    pin = part[pl.ds(pl.multiple_of(sec * rows, rows), rows), :] + opart[...]
    pin_out[...] = pin
    inv = lax.rsqrt(jnp.sum(pin * pin, axis=1, keepdims=True) + EPSILON)
    q_out[me] = (pin * inv).astype(BF16)
    each_peer(n, me, lambda p, i: remote(
        q_out.at[me], q_out.at[me], sq.at[i], rq.at[me], shard=p).start())
    each_peer(n, me, lambda p, i: remote(
        tab.at[p], tab_out.at[p], st.at[i], rt.at[p], shard=p).wait())
    got = tab_out[...]
    count = jnp.sum(got[:, 3, :], axis=1, keepdims=True)
    codes = jnp.where(iota((n, LANES), 1) == LANES - 1, count, got[:, 0, :])
    code_out[...] = (codes + 0.5).astype(jnp.int32)
    prob_out[...] = got[:, 1, :]
    teach_out[...] = got[:, 2, :]
    each_peer(n, me, lambda p, i: remote(
        q_out.at[me], q_out.at[p], sq.at[i], rq.at[p], shard=p).wait())


def score_kernel(
    n, half_q, nt, slot_bits, query_bits,
    code, prob, teach, plen, q_ref, pas_hbm, a_out, t_out, stat_out,
    pas, turned, u_ref, stud_ref, own_ref, prob_ref, teach_ref, coef_ref, listing, sem,
):
    load = pltpu.make_async_copy(pas_hbm, pas, sem)
    load.start()
    pass_tokens = pas.shape[1]
    scale = SHARPNESS * math.log2(math.e)
    len_bits = nt.bit_length()
    high = slot_bits + query_bits + len_bits

    def per_source(q, start):
        cnt = code[q, LANES - 1]

        def eight(g, carry):
            for k in range(8):
                r = g * 8 + k
                e = start + r
                listing[e] = code[q, r] | lax.shift_left(q, high)
                prob_ref[pl.ds(e, 1), :] = jnp.full((1, LANES), prob[q, r], F32)
                teach_ref[pl.ds(e, 1), :] = jnp.full((1, LANES), teach[q, r], F32)
            return carry

        lax.fori_loop(0, lax.shift_right_logical(cnt + 7, 3), eight, 0)
        return start + cnt

    count = lax.fori_loop(0, n, per_source, 0)
    for k in range(GROUP):
        listing[count + k] = 0
    groups = lax.div(count + (GROUP - 1), GROUP)
    side = LANES // nt
    tok = iota((pass_tokens, LANES), 0)
    lane = iota((1, LANES), 1)
    piece = iota((LANES, LANES), 1)

    def place(c):
        which = lax.shift_right_logical(c, slot_bits) & ((1 << query_bits) - 1)
        return lax.shift_right_logical(c, high), which

    def turn(q, carry):
        for j in range(half_q):
            vecs = q_ref[q, j * nt : (j + 1) * nt, :].astype(F32)
            turned[q * half_q + j] = jnp.concatenate([vecs] * side, axis=0).T.astype(BF16)
        return carry

    lax.fori_loop(0, n, turn, 0)
    load.wait()

    def group(g, carry):
        for first in range(0, GROUP, side):
            blocks, weights, owners = [], [], []
            limit, tokens = jnp.zeros((1, LANES), jnp.int32), jnp.zeros((1, LANES), jnp.int32)
            for k in range(side):
                c = listing[g * GROUP + first + k]
                slot = jnp.maximum((c & ((1 << slot_bits) - 1)) - 1, 0)
                q, which = place(c)
                qlen = lax.shift_right_logical(c, slot_bits + query_bits) & ((1 << len_bits) - 1)
                owners.append(q * half_q + which)
                blocks.append(pas[slot])
                here = (piece >= k * nt) & (piece < (k + 1) * nt)
                weights.append(jnp.where(here, turned[owners[k]], jnp.zeros((), BF16)))
                here = lane >= k * nt
                limit = jnp.where(here, plen[slot], limit)
                tokens = jnp.where(here, qlen + k * nt, tokens)
            logits = jnp.dot(
                jnp.concatenate(blocks, axis=1), jnp.concatenate(weights, axis=0),
                preferred_element_type=F32,
            )
            logits = jnp.where(tok < limit, logits * scale, NEGATIVE)
            top = jnp.max(logits, axis=0, keepdims=True)
            terms = jnp.exp2(logits - top)
            total = jnp.sum(terms, axis=0, keepdims=True)
            best = top * (math.log(2.0) / SHARPNESS) + jnp.log(total) * (1.0 / SHARPNESS)
            best = jnp.where(lane < tokens, best, 0.0)
            shares = (terms * (1.0 / total)).T.astype(BF16)
            for k in range(side):
                e = g * GROUP + first + k
                here = (lane >= k * nt) & (lane < (k + 1) * nt)
                student = jnp.sum(jnp.where(here, best, 0.0), axis=1, keepdims=True)
                u_ref[e] = jnp.dot(
                    shares[k * nt : (k + 1) * nt, :], blocks[k], preferred_element_type=F32
                )
                stud_ref[pl.ds(e, 1), :] = jnp.broadcast_to(student, (1, LANES))
                own_ref[pl.ds(e, 1), :] = jnp.full((1, LANES), owners[k], jnp.int32)
        return carry

    lax.fori_loop(0, groups, group, 0)

    width = stat_out.shape[1]
    chunks = lax.div(count + (CHUNK - 1), CHUNK)

    def wide(x):
        return x if width == LANES else jnp.concatenate([x] * (width // LANES), axis=1)

    def chunk(c):
        at = pl.ds(pl.multiple_of(c * CHUNK, CHUNK), CHUNK)
        valid = iota((CHUNK, 1), 0) + c * CHUNK < count
        mask = (wide(own_ref[at, :]) == iota((CHUNK, width), 1)) & valid
        return at, valid, mask, stud_ref[at, :]

    def find_top(c, top):
        at, valid, mask, stud = chunk(c)
        return jnp.maximum(
            top, jnp.max(jnp.where(mask, wide(stud), NEGATIVE), axis=0, keepdims=True)
        )

    none = jnp.zeros((1, width), F32)
    top = lax.fori_loop(0, chunks, find_top, none + NEGATIVE)

    def weigh(c, sums):
        at, valid, mask, stud = chunk(c)
        mine = jnp.max(jnp.where(mask, top, NEGATIVE), axis=1, keepdims=True)
        terms = jnp.where(valid, jnp.exp(jnp.where(valid, stud - mine, 0.0)), 0.0)
        likely = jnp.where(valid, prob_ref[at, :], 0.0)
        coef_ref[at, :] = terms
        cross = jnp.where(valid, likely * (teach_ref[at, :] - stud), 0.0)
        prob_ref[at, :] = likely
        return (
            sums[0] + jnp.sum(jnp.where(mask, wide(terms), 0.0), axis=0, keepdims=True),
            sums[1] + jnp.sum(jnp.where(mask, wide(cross), 0.0), axis=0, keepdims=True),
        )

    total, cross = lax.fori_loop(0, chunks, weigh, (none, none))
    stat_out[...] = jnp.concatenate([top, total, cross, jnp.zeros((5, width), F32)], axis=0)
    a_out[...] = jnp.zeros_like(a_out)
    t_out[...] = jnp.zeros_like(t_out)

    def gather(g, carry):
        for k in range(4):
            e = g * 4 + k
            q, which = place(listing[e])
            at = q * half_q + which
            unit = u_ref[e]
            a_out[at] += coef_ref[pl.ds(e, 1), :] * unit
            t_out[at] += prob_ref[pl.ds(e, 1), :] * unit
        return carry

    lax.fori_loop(0, lax.shift_right_logical(count + 3, 2), gather, 0)


def grad_kernel(
    n, half_q, nt, inside, qlen, a_ref, t_ref, stat_ref, pin_ref, info_ref, h_ref, p_ref,
    kl_out, gh_out, gp_out,
    stats, crow, psend, rpart, ing, klbuf, lp, rs,
    sib_send, sib_recv, s0, r0, s1, r1, s2, r2, s3, r3,
):
    sec, me = lax.axis_index("section"), lax.axis_index("shard")
    rows = half_q * nt
    width = stat_ref.shape[1]
    enter(n, me, sec)
    each_peer(n, me, lambda p, i: remote(
        stat_ref, stats.at[me], s0.at[i], r0.at[me], shard=p).start())
    stats[me] = stat_ref[...]
    each_peer(n, me, lambda p, i: remote(
        stat_ref, stats.at[p], s0.at[i], r0.at[p], shard=p).wait())
    tops, totals, crosses = stats[:, 0, :], stats[:, 1, :], stats[:, 2, :]
    top = jnp.max(tops, axis=0, keepdims=True)
    lse = top + jnp.log(jnp.sum(totals * jnp.exp(tops - top), axis=0, keepdims=True))
    cross = jnp.sum(crosses, axis=0, keepdims=True)
    factor = jnp.exp(stat_ref[0:1, :] - lse)
    count = crow.shape[0]
    crow[...] = jnp.broadcast_to(
        jnp.sum(
            jnp.where(iota((count, width), 0) == iota((count, width), 1), factor, 0.0),
            axis=1, keepdims=True,
        ),
        crow.shape,
    )

    def make_part(p):
        for j in range(half_q):
            at = p * half_q + j
            value = a_ref[at] * crow[pl.ds(at, 1), :] - t_ref[at]
            psend[p, j * nt : (j + 1) * nt, :] = value.astype(BF16)

    def send_part(p, i):
        make_part(p)
        remote(psend.at[p], rpart.at[me], s1.at[i], r1.at[me], shard=p).start()

    each_peer(n, me, send_part)
    make_part(me)
    rpart[me] = psend[me]

    kl = jnp.zeros((8, LANES), F32)
    lane = iota((1, width), 1)
    for j in range(half_q):
        mine = jnp.sum(jnp.where(lane == me * half_q + j, cross + lse, 0.0), axis=1, keepdims=True)
        kl = jnp.where(
            iota((8, LANES), 1) == sec * half_q + j, mine - info_ref[0:1, j : j + 1], kl
        )
    klbuf[sec] = kl
    kl_copy = remote(klbuf.at[sec], klbuf.at[sec], sib_send.at[0], sib_recv.at[0], section=1 - sec)
    kl_copy.start()
    pin = pin_ref[...]
    inv = lax.rsqrt(jnp.sum(pin * pin, axis=1, keepdims=True) + EPSILON)

    each_peer(n, me, lambda p, i: remote(
        psend.at[p], rpart.at[p], s1.at[i], r1.at[p], shard=p).wait())
    vec = lax.fori_loop(
        0, n, lambda o, total: total + rpart[o].astype(F32), jnp.zeros((rows, LANES), F32)
    )
    tok = iota((nt, LANES), 0)
    vec = jnp.concatenate(
        [
            jnp.where(tok < qlen[sec * half_q + j], vec[j * nt : (j + 1) * nt, :], 0.0)
            for j in range(half_q)
        ],
        axis=0,
    )
    grad = inv * vec - inv * inv * inv * pin * jnp.sum(pin * vec, axis=1, keepdims=True)
    own = pl.ds(pl.multiple_of(sec * rows, rows), rows)
    ing[own, :] = grad.astype(BF16)
    in_copy = remote(ing.at[own], ing.at[own], sib_send.at[1], sib_recv.at[1], section=1 - sec)
    in_copy.start()
    kl_copy.wait()
    kl_out[...] = klbuf[0] + klbuf[1]
    in_copy.wait()
    flat = ing[...]
    terms = lax.dot_general(
        h_ref[...], flat, (((0,), (0,)), ((), ())), preferred_element_type=F32
    )
    if inside:
        lp[...] = terms
        piece = terms.shape[0] // n

        def span(p):
            return pl.ds(pl.multiple_of(p * piece, 8), piece)

        each_peer(n, me, lambda p, i: remote(
            lp.at[span(p)], rs.at[me], s2.at[i], r2.at[me], shard=p).start())
        rs[me] = lp[span(me), :]
    else:
        gp_out[...] = terms
    gh_out[...] = lax.dot_general(
        flat, p_ref[...], (((1,), (1,)), ((), ())), preferred_element_type=F32
    ).astype(BF16)
    if inside:
        each_peer(n, me, lambda p, i: remote(
            lp.at[span(p)], rs.at[p], s2.at[i], r2.at[p], shard=p).wait())
        gp_out[span(me), :] = jnp.sum(rs[...], axis=0)
        each_peer(n, me, lambda p, i: remote(
            gp_out.at[span(me)], gp_out.at[span(me)], s3.at[i], r3.at[me], shard=p).start())
        each_peer(n, me, lambda p, i: remote(
            gp_out.at[span(me)], gp_out.at[span(p)], s3.at[i], r3.at[p], shard=p).wait())


def local(hidden, proj, passages, pass_len, query_len, cand_owner, cand_slot, teacher):
    nq, nt, feat = hidden.shape
    dv = proj.shape[1]
    slots, pass_tokens, _ = passages.shape
    n = lax.axis_size("shard")
    half_q = nq // 2
    rows = half_q * nt
    requests = cand_owner.size
    cap = 2 * max(2, (2 * requests + n - 1) // n)
    most = -(-(n * cap + 8) // CHUNK) * CHUNK
    slot_bits = slots.bit_length()
    query_bits = max(1, (half_q - 1).bit_length())
    width = -(-(n * half_q) // LANES) * LANES
    flat_h = hidden.reshape(nq * nt, feat)

    query = jnp.broadcast_to(jnp.arange(nq)[:, None], teacher.shape)
    code = (
        cand_slot.reshape(teacher.shape)
        + 1
        + ((query % half_q) << slot_bits)
        + (query_len[:, None] << (slot_bits + query_bits))
    )
    zero = jnp.zeros((requests,), F32)
    meta = jnp.stack(
        [
            cand_owner.reshape(-1).astype(F32),
            code.reshape(-1).astype(F32),
            teacher.reshape(-1),
            query.reshape(-1).astype(F32),
            zero, zero, zero, zero,
        ]
    )
    vmem = pl.BlockSpec(memory_space=pltpu.VMEM)
    smem = pl.BlockSpec(memory_space=pltpu.SMEM)
    dma = pltpu.SemaphoreType.DMA
    shape = jax.ShapeDtypeStruct
    q_all, pin, codes, probs, teachs, info = pl.pallas_call(
        functools.partial(request_kernel, n, half_q, nt),
        out_shape=(
            shape((n, rows, dv), BF16),
            shape((rows, dv), F32),
            shape((n, LANES), jnp.int32),
            shape((n, LANES), F32),
            shape((n, LANES), F32),
            shape((8, LANES), F32),
        ),
        in_specs=[vmem] * 3,
        out_specs=(vmem,) * 6,
        scratch_shapes=[
            pltpu.VMEM((n, 8, LANES), F32),
            pltpu.VMEM((nq * nt, dv), F32),
            pltpu.VMEM((rows, dv), F32),
            pltpu.VMEM((8, requests), F32),
            pltpu.VMEM((n, 8, LANES), F32),
            dma((2,)), dma((2,)), dma((n,)), dma((n,)), dma((n,)), dma((n,)),
        ],
        compiler_params=pltpu.CompilerParams(
            collective_id=0, has_side_effects=True, vmem_limit_bytes=32 << 20
        ),
        name="requests",
    )(flat_h, proj, meta)

    a_part, t_part, stat = pl.pallas_call(
        functools.partial(score_kernel, n, half_q, nt, slot_bits, query_bits),
        out_shape=(
            shape((n * half_q, nt, dv), F32),
            shape((n * half_q, nt, dv), F32),
            shape((8, width), F32),
        ),
        in_specs=[smem] * 4 + [vmem, pl.BlockSpec(memory_space=pl.ANY)],
        out_specs=(vmem,) * 3,
        scratch_shapes=[
            pltpu.VMEM((slots, pass_tokens, dv), BF16),
            pltpu.VMEM((n * half_q, dv, LANES), BF16),
            pltpu.VMEM((most, nt, dv), F32),
            pltpu.VMEM((most, LANES), F32),
            pltpu.VMEM((most, LANES), jnp.int32),
            pltpu.VMEM((most, LANES), F32),
            pltpu.VMEM((most, LANES), F32),
            pltpu.VMEM((most, LANES), F32),
            pltpu.SMEM((most,), jnp.int32),
            dma,
        ],
        compiler_params=pltpu.CompilerParams(vmem_limit_bytes=48 << 20),
        name="scores",
    )(codes, probs, teachs, pass_len, q_all, passages)

    inside = feat % n == 0 and (feat // n) % 8 == 0
    piece = feat // n if inside else 8
    kl, gh, gp = pl.pallas_call(
        functools.partial(grad_kernel, n, half_q, nt, inside),
        out_shape=(
            shape((8, LANES), F32),
            shape((nq * nt, feat), BF16),
            shape((feat, dv), F32),
        ),
        in_specs=[smem] + [vmem] * 7,
        out_specs=(vmem,) * 3,
        scratch_shapes=[
            pltpu.VMEM((n, 8, width), F32),
            pltpu.VMEM((n * half_q, LANES), F32),
            pltpu.VMEM((n, rows, dv), BF16),
            pltpu.VMEM((n, rows, dv), BF16),
            pltpu.VMEM((nq * nt, dv), BF16),
            pltpu.VMEM((2, 8, LANES), F32),
            pltpu.VMEM((feat, dv), F32),
            pltpu.VMEM((n, piece, dv), F32),
            dma((2,)), dma((2,)),
        ]
        + [dma((n,))] * 8,
        compiler_params=pltpu.CompilerParams(
            collective_id=1, has_side_effects=True, vmem_limit_bytes=48 << 20
        ),
        name="grads",
    )(query_len, a_part, t_part, stat, pin, info, flat_h, proj)
    if not inside:
        gp = lax.psum(gp, "shard")
    return kl[0, :nq], gh.reshape(nq, nt, feat), gp


def solution(mesh):
    in_specs = (
        P("shard", None, "section"),
        P("section", None),
        P("shard", None, None),
        P("shard"),
        P("shard"),
        P("section", "shard", None, None),
        P("section", "shard", None),
        P("shard", "section"),
    )
    out_specs = (P("shard"), P("shard", None, "section"), P("section", None))
    return jax.shard_map(local, mesh=mesh, in_specs=in_specs, out_specs=out_specs, check_vma=False)
```

```python
import functools
import math

import jax
import jax.numpy as jnp
from jax import lax
from jax.experimental import pallas as pl
from jax.experimental.pallas import tpu as pltpu
from jax.sharding import PartitionSpec as P

SHARPNESS = 64.0
EPSILON = 1e-06
NEGATIVE = -1e30
LANES = 128
GROUP = 16
CHUNK = 64
F32 = jnp.float32
BF16 = jnp.bfloat16
MESH = pl.DeviceIdType.MESH


def iota(shape, axis):
    return lax.broadcasted_iota(jnp.int32, shape, axis)


def remote(src, dst, send, recv, **where):
    return pltpu.make_async_remote_copy(
        src_ref=src, dst_ref=dst, send_sem=send, recv_sem=recv, device_id=where, device_id_type=MESH
    )


def enter(n, me, sec):
    barrier = pltpu.get_barrier_semaphore()
    pl.semaphore_signal(barrier, inc=1, device_id={"section": 1 - sec}, device_id_type=MESH)

    def greet(i, carry):
        pl.semaphore_signal(
            barrier, inc=1, device_id={"shard": lax.rem(me + i, n)}, device_id_type=MESH
        )
        return carry

    lax.fori_loop(1, n, greet, 0)
    pl.semaphore_wait(barrier, n)


def each_peer(n, me, body):
    def step(i, carry):
        body(lax.rem(me + i, n), i)
        return carry

    lax.fori_loop(1, n, step, 0)


def request_kernel(
    n, half_q, nt, h_ref, p_ref, meta_ref,
    q_out, pin_out, code_out, prob_out, teach_out, info_out,
    tab_out, part, opart, ometa, tab,
    sib_send, sib_recv, st, rt, sq, rq,
):
    sec, me = lax.axis_index("section"), lax.axis_index("shard")
    rows = half_q * nt
    enter(n, me, sec)
    meta_copy = remote(meta_ref, ometa, sib_send.at[0], sib_recv.at[0], section=1 - sec)
    meta_copy.start()
    part[...] = jnp.dot(h_ref[...], p_ref[...], preferred_element_type=F32)
    other_rows = pl.ds(pl.multiple_of((1 - sec) * rows, rows), rows)
    part_copy = remote(part.at[other_rows], opart, sib_send.at[1], sib_recv.at[1], section=1 - sec)
    part_copy.start()
    meta_copy.wait()

    width = meta_ref.shape[1]
    meta = jnp.concatenate([meta_ref[...], ometa[...]], axis=1)
    owner = meta[0:1, :].astype(jnp.int32)
    code, teach = meta[1:2, :], meta[2:3, :]
    query = meta[3:4, :].astype(jnp.int32)
    valid = (query >= sec * half_q) & (query < (sec + 1) * half_q)
    prob = jnp.zeros_like(teach)
    lane = iota((8, LANES), 1)
    info = jnp.zeros((8, LANES), F32)
    for j in range(half_q):
        mask = query == sec * half_q + j
        top = jnp.max(jnp.where(mask, teach, NEGATIVE), axis=1, keepdims=True)
        terms = jnp.where(mask, jnp.exp(jnp.where(mask, teach - top, 0.0)), 0.0)
        total = jnp.sum(terms, axis=1, keepdims=True)
        prob = prob + terms / total
        info = jnp.where(lane == j, top + jnp.log(total), info)
    info_out[...] = info
    named = jnp.where((iota((n, 2 * width), 0) == owner) & valid, 1.0, 0.0)
    before = jnp.where(iota((2 * width, 2 * width), 0) < iota((2 * width, 2 * width), 1), 1.0, 0.0)
    counts = jnp.dot(named.astype(BF16), before.astype(BF16), preferred_element_type=F32)
    rank = jnp.sum(named * counts, axis=0, keepdims=True).astype(jnp.int32)
    at_rank = jnp.where((iota((LANES, 2 * width), 0) == rank) & valid, 1.0, 0.0)
    line = iota((n * 8, 2 * width), 0)
    kind = line & 7
    value = jnp.where(kind == 0, code, jnp.where(kind == 1, prob, jnp.where(kind == 2, teach, 1.0)))
    value = jnp.where((lax.shift_right_logical(line, 3) == owner) & valid & (kind < 4), value, 0.0)
    table = lax.dot_general(
        value, at_rank, (((1,), (1,)), ((), ())),
        precision=lax.Precision.HIGHEST, preferred_element_type=F32,
    )
    tab[...] = table.reshape(n, 8, LANES)
    each_peer(n, me, lambda p, i: remote(
        tab.at[p], tab_out.at[me], st.at[i], rt.at[me], shard=p).start())
    tab_out[me] = tab[me]

    part_copy.wait()
    pin = part[pl.ds(pl.multiple_of(sec * rows, rows), rows), :] + opart[...]
    pin_out[...] = pin
    inv = lax.rsqrt(jnp.sum(pin * pin, axis=1, keepdims=True) + EPSILON)
    q_out[me] = (pin * inv).astype(BF16)
    each_peer(n, me, lambda p, i: remote(
        q_out.at[me], q_out.at[me], sq.at[i], rq.at[me], shard=p).start())
    each_peer(n, me, lambda p, i: remote(
        tab.at[p], tab_out.at[p], st.at[i], rt.at[p], shard=p).wait())
    got = tab_out[...]
    count = jnp.sum(got[:, 3, :], axis=1, keepdims=True)
    codes = jnp.where(iota((n, LANES), 1) == LANES - 1, count, got[:, 0, :])
    code_out[...] = (codes + 0.5).astype(jnp.int32)
    prob_out[...] = got[:, 1, :]
    teach_out[...] = got[:, 2, :]
    each_peer(n, me, lambda p, i: remote(
        q_out.at[me], q_out.at[p], sq.at[i], rq.at[p], shard=p).wait())


def score_kernel(
    n, half_q, nt, slot_bits, query_bits,
    code, prob, teach, plen, q_ref, pas_hbm, a_out, t_out, stat_out,
    pas, turned, u_ref, stud_ref, own_ref, prob_ref, teach_ref, coef_ref, listing, sem,
):
    load = pltpu.make_async_copy(pas_hbm, pas, sem)
    load.start()
    pass_tokens = pas.shape[1]
    scale = SHARPNESS * math.log2(math.e)
    len_bits = nt.bit_length()
    high = slot_bits + query_bits + len_bits

    def per_source(q, start):
        cnt = code[q, LANES - 1]

        def eight(g, carry):
            for k in range(8):
                r = g * 8 + k
                e = start + r
                listing[e] = code[q, r] | lax.shift_left(q, high)
                prob_ref[pl.ds(e, 1), :] = jnp.full((1, LANES), prob[q, r], F32)
                teach_ref[pl.ds(e, 1), :] = jnp.full((1, LANES), teach[q, r], F32)
            return carry

        lax.fori_loop(0, lax.shift_right_logical(cnt + 7, 3), eight, 0)
        return start + cnt

    count = lax.fori_loop(0, n, per_source, 0)
    for k in range(GROUP):
        listing[count + k] = 0
    groups = lax.div(count + (GROUP - 1), GROUP)
    side = LANES // nt
    tok = iota((pass_tokens, LANES), 0)
    lane = iota((1, LANES), 1)
    piece = iota((LANES, LANES), 1)

    def place(c):
        which = lax.shift_right_logical(c, slot_bits) & ((1 << query_bits) - 1)
        return lax.shift_right_logical(c, high), which

    def turn(q, carry):
        for j in range(half_q):
            vecs = q_ref[q, j * nt : (j + 1) * nt, :].astype(F32)
            turned[q * half_q + j] = jnp.concatenate([vecs] * side, axis=0).T.astype(BF16)
        return carry

    lax.fori_loop(0, n, turn, 0)
    load.wait()

    def group(g, carry):
        for first in range(0, GROUP, side):
            blocks, weights, owners = [], [], []
            limit, tokens = jnp.zeros((1, LANES), jnp.int32), jnp.zeros((1, LANES), jnp.int32)
            for k in range(side):
                c = listing[g * GROUP + first + k]
                slot = jnp.maximum((c & ((1 << slot_bits) - 1)) - 1, 0)
                q, which = place(c)
                qlen = lax.shift_right_logical(c, slot_bits + query_bits) & ((1 << len_bits) - 1)
                owners.append(q * half_q + which)
                blocks.append(pas[slot])
                here = (piece >= k * nt) & (piece < (k + 1) * nt)
                weights.append(jnp.where(here, turned[owners[k]], jnp.zeros((), BF16)))
                here = lane >= k * nt
                limit = jnp.where(here, plen[slot], limit)
                tokens = jnp.where(here, qlen + k * nt, tokens)
            logits = jnp.dot(
                jnp.concatenate(blocks, axis=1), jnp.concatenate(weights, axis=0),
                preferred_element_type=F32,
            )
            logits = jnp.where(tok < limit, logits * scale, NEGATIVE)
            top = jnp.max(logits, axis=0, keepdims=True)
            terms = jnp.exp2(logits - top)
            total = jnp.sum(terms, axis=0, keepdims=True)
            best = top * (math.log(2.0) / SHARPNESS) + jnp.log(total) * (1.0 / SHARPNESS)
            best = jnp.where(lane < tokens, best, 0.0)
            shares = (terms * (1.0 / total)).astype(BF16).T
            for k in range(side):
                e = g * GROUP + first + k
                here = (lane >= k * nt) & (lane < (k + 1) * nt)
                student = jnp.sum(jnp.where(here, best, 0.0), axis=1, keepdims=True)
                u_ref[e] = jnp.dot(
                    shares[k * nt : (k + 1) * nt, :], blocks[k], preferred_element_type=F32
                )
                stud_ref[pl.ds(e, 1), :] = jnp.broadcast_to(student, (1, LANES))
                own_ref[pl.ds(e, 1), :] = jnp.full((1, LANES), owners[k], jnp.int32)
        return carry

    lax.fori_loop(0, groups, group, 0)

    width = stat_out.shape[1]
    chunks = lax.div(count + (CHUNK - 1), CHUNK)

    def wide(x):
        return x if width == LANES else jnp.concatenate([x] * (width // LANES), axis=1)

    def chunk(c):
        at = pl.ds(pl.multiple_of(c * CHUNK, CHUNK), CHUNK)
        valid = iota((CHUNK, 1), 0) + c * CHUNK < count
        mask = (wide(own_ref[at, :]) == iota((CHUNK, width), 1)) & valid
        return at, valid, mask, stud_ref[at, :]

    def find_top(c, top):
        at, valid, mask, stud = chunk(c)
        return jnp.maximum(
            top, jnp.max(jnp.where(mask, wide(stud), NEGATIVE), axis=0, keepdims=True)
        )

    none = jnp.zeros((1, width), F32)
    top = lax.fori_loop(0, chunks, find_top, none + NEGATIVE)

    def weigh(c, sums):
        at, valid, mask, stud = chunk(c)
        mine = jnp.max(jnp.where(mask, top, NEGATIVE), axis=1, keepdims=True)
        terms = jnp.where(valid, jnp.exp(jnp.where(valid, stud - mine, 0.0)), 0.0)
        likely = jnp.where(valid, prob_ref[at, :], 0.0)
        coef_ref[at, :] = terms
        cross = jnp.where(valid, likely * (teach_ref[at, :] - stud), 0.0)
        prob_ref[at, :] = likely
        return (
            sums[0] + jnp.sum(jnp.where(mask, wide(terms), 0.0), axis=0, keepdims=True),
            sums[1] + jnp.sum(jnp.where(mask, wide(cross), 0.0), axis=0, keepdims=True),
        )

    total, cross = lax.fori_loop(0, chunks, weigh, (none, none))
    stat_out[...] = jnp.concatenate([top, total, cross, jnp.zeros((5, width), F32)], axis=0)
    a_out[...] = jnp.zeros_like(a_out)
    t_out[...] = jnp.zeros_like(t_out)

    def gather(g, carry):
        for k in range(4):
            e = g * 4 + k
            q, which = place(listing[e])
            at = q * half_q + which
            unit = u_ref[e]
            a_out[at] += coef_ref[pl.ds(e, 1), :] * unit
            t_out[at] += prob_ref[pl.ds(e, 1), :] * unit
        return carry

    lax.fori_loop(0, lax.shift_right_logical(count + 3, 2), gather, 0)


def grad_kernel(
    n, half_q, nt, inside, qlen, a_ref, t_ref, stat_ref, pin_ref, info_ref, h_ref, p_ref,
    kl_out, gh_out, gp_out,
    stats, crow, psend, rpart, ing, klbuf, lp, rs,
    sib_send, sib_recv, s0, r0, s1, r1, s2, r2, s3, r3,
):
    sec, me = lax.axis_index("section"), lax.axis_index("shard")
    rows = half_q * nt
    width = stat_ref.shape[1]
    enter(n, me, sec)
    each_peer(n, me, lambda p, i: remote(
        stat_ref, stats.at[me], s0.at[i], r0.at[me], shard=p).start())
    stats[me] = stat_ref[...]
    each_peer(n, me, lambda p, i: remote(
        stat_ref, stats.at[p], s0.at[i], r0.at[p], shard=p).wait())
    tops, totals, crosses = stats[:, 0, :], stats[:, 1, :], stats[:, 2, :]
    top = jnp.max(tops, axis=0, keepdims=True)
    lse = top + jnp.log(jnp.sum(totals * jnp.exp(tops - top), axis=0, keepdims=True))
    cross = jnp.sum(crosses, axis=0, keepdims=True)
    factor = jnp.exp(stat_ref[0:1, :] - lse)
    count = crow.shape[0]
    crow[...] = jnp.broadcast_to(
        jnp.sum(
            jnp.where(iota((count, width), 0) == iota((count, width), 1), factor, 0.0),
            axis=1, keepdims=True,
        ),
        crow.shape,
    )

    def make_part(p):
        for j in range(half_q):
            at = p * half_q + j
            value = a_ref[at] * crow[pl.ds(at, 1), :] - t_ref[at]
            psend[p, j * nt : (j + 1) * nt, :] = value.astype(BF16)

    def send_part(p, i):
        make_part(p)
        remote(psend.at[p], rpart.at[me], s1.at[i], r1.at[me], shard=p).start()

    each_peer(n, me, send_part)
    make_part(me)
    rpart[me] = psend[me]

    kl = jnp.zeros((8, LANES), F32)
    lane = iota((1, width), 1)
    for j in range(half_q):
        mine = jnp.sum(jnp.where(lane == me * half_q + j, cross + lse, 0.0), axis=1, keepdims=True)
        kl = jnp.where(
            iota((8, LANES), 1) == sec * half_q + j, mine - info_ref[0:1, j : j + 1], kl
        )
    klbuf[sec] = kl
    kl_copy = remote(klbuf.at[sec], klbuf.at[sec], sib_send.at[0], sib_recv.at[0], section=1 - sec)
    kl_copy.start()
    pin = pin_ref[...]
    inv = lax.rsqrt(jnp.sum(pin * pin, axis=1, keepdims=True) + EPSILON)

    each_peer(n, me, lambda p, i: remote(
        psend.at[p], rpart.at[p], s1.at[i], r1.at[p], shard=p).wait())
    vec = lax.fori_loop(
        0, n, lambda o, total: total + rpart[o].astype(F32), jnp.zeros((rows, LANES), F32)
    )
    tok = iota((nt, LANES), 0)
    vec = jnp.concatenate(
        [
            jnp.where(tok < qlen[sec * half_q + j], vec[j * nt : (j + 1) * nt, :], 0.0)
            for j in range(half_q)
        ],
        axis=0,
    )
    grad = inv * vec - inv * inv * inv * pin * jnp.sum(pin * vec, axis=1, keepdims=True)
    own = pl.ds(pl.multiple_of(sec * rows, rows), rows)
    ing[own, :] = grad.astype(BF16)
    in_copy = remote(ing.at[own], ing.at[own], sib_send.at[1], sib_recv.at[1], section=1 - sec)
    in_copy.start()
    kl_copy.wait()
    kl_out[...] = klbuf[0] + klbuf[1]
    in_copy.wait()
    flat = ing[...]
    terms = lax.dot_general(
        h_ref[...], flat, (((0,), (0,)), ((), ())), preferred_element_type=F32
    )
    if inside:
        lp[...] = terms
        piece = terms.shape[0] // n

        def span(p):
            return pl.ds(pl.multiple_of(p * piece, 8), piece)

        each_peer(n, me, lambda p, i: remote(
            lp.at[span(p)], rs.at[me], s2.at[i], r2.at[me], shard=p).start())
        rs[me] = lp[span(me), :]
    else:
        gp_out[...] = terms
    gh_out[...] = lax.dot_general(
        flat, p_ref[...], (((1,), (1,)), ((), ())), preferred_element_type=F32
    ).astype(BF16)
    if inside:
        each_peer(n, me, lambda p, i: remote(
            lp.at[span(p)], rs.at[p], s2.at[i], r2.at[p], shard=p).wait())
        gp_out[span(me), :] = jnp.sum(rs[...], axis=0)
        each_peer(n, me, lambda p, i: remote(
            gp_out.at[span(me)], gp_out.at[span(me)], s3.at[i], r3.at[me], shard=p).start())
        each_peer(n, me, lambda p, i: remote(
            gp_out.at[span(me)], gp_out.at[span(p)], s3.at[i], r3.at[p], shard=p).wait())


def local(hidden, proj, passages, pass_len, query_len, cand_owner, cand_slot, teacher):
    nq, nt, feat = hidden.shape
    dv = proj.shape[1]
    slots, pass_tokens, _ = passages.shape
    n = lax.axis_size("shard")
    half_q = nq // 2
    rows = half_q * nt
    requests = cand_owner.size
    cap = 2 * max(2, (2 * requests + n - 1) // n)
    most = -(-(n * cap + GROUP) // CHUNK) * CHUNK
    slot_bits = slots.bit_length()
    query_bits = max(1, (half_q - 1).bit_length())
    width = -(-(n * half_q) // LANES) * LANES
    flat_h = hidden.reshape(nq * nt, feat)

    query = jnp.broadcast_to(jnp.arange(nq)[:, None], teacher.shape)
    code = (
        cand_slot.reshape(teacher.shape)
        + 1
        + ((query % half_q) << slot_bits)
        + (query_len[:, None] << (slot_bits + query_bits))
    )
    zero = jnp.zeros((requests,), F32)
    meta = jnp.stack(
        [
            cand_owner.reshape(-1).astype(F32),
            code.reshape(-1).astype(F32),
            teacher.reshape(-1),
            query.reshape(-1).astype(F32),
            zero, zero, zero, zero,
        ]
    )
    vmem = pl.BlockSpec(memory_space=pltpu.VMEM)
    smem = pl.BlockSpec(memory_space=pltpu.SMEM)
    dma = pltpu.SemaphoreType.DMA
    shape = jax.ShapeDtypeStruct
    q_all, pin, codes, probs, teachs, info = pl.pallas_call(
        functools.partial(request_kernel, n, half_q, nt),
        out_shape=(
            shape((n, rows, dv), BF16),
            shape((rows, dv), F32),
            shape((n, LANES), jnp.int32),
            shape((n, LANES), F32),
            shape((n, LANES), F32),
            shape((8, LANES), F32),
        ),
        in_specs=[vmem] * 3,
        out_specs=(vmem,) * 6,
        scratch_shapes=[
            pltpu.VMEM((n, 8, LANES), F32),
            pltpu.VMEM((nq * nt, dv), F32),
            pltpu.VMEM((rows, dv), F32),
            pltpu.VMEM((8, requests), F32),
            pltpu.VMEM((n, 8, LANES), F32),
            dma((2,)), dma((2,)), dma((n,)), dma((n,)), dma((n,)), dma((n,)),
        ],
        compiler_params=pltpu.CompilerParams(
            collective_id=0, has_side_effects=True, vmem_limit_bytes=32 << 20
        ),
        name="requests",
    )(flat_h, proj, meta)

    a_part, t_part, stat = pl.pallas_call(
        functools.partial(score_kernel, n, half_q, nt, slot_bits, query_bits),
        out_shape=(
            shape((n * half_q, nt, dv), F32),
            shape((n * half_q, nt, dv), F32),
            shape((8, width), F32),
        ),
        in_specs=[smem] * 4 + [vmem, pl.BlockSpec(memory_space=pl.ANY)],
        out_specs=(vmem,) * 3,
        scratch_shapes=[
            pltpu.VMEM((slots, pass_tokens, dv), BF16),
            pltpu.VMEM((n * half_q, dv, LANES), BF16),
            pltpu.VMEM((most, nt, dv), F32),
            pltpu.VMEM((most, LANES), F32),
            pltpu.VMEM((most, LANES), jnp.int32),
            pltpu.VMEM((most, LANES), F32),
            pltpu.VMEM((most, LANES), F32),
            pltpu.VMEM((most, LANES), F32),
            pltpu.SMEM((most,), jnp.int32),
            dma,
        ],
        compiler_params=pltpu.CompilerParams(vmem_limit_bytes=48 << 20),
        name="scores",
    )(codes, probs, teachs, pass_len, q_all, passages)

    inside = feat % n == 0 and (feat // n) % 8 == 0
    piece = feat // n if inside else 8
    kl, gh, gp = pl.pallas_call(
        functools.partial(grad_kernel, n, half_q, nt, inside),
        out_shape=(
            shape((8, LANES), F32),
            shape((nq * nt, feat), BF16),
            shape((feat, dv), F32),
        ),
        in_specs=[smem] + [vmem] * 7,
        out_specs=(vmem,) * 3,
        scratch_shapes=[
            pltpu.VMEM((n, 8, width), F32),
            pltpu.VMEM((n * half_q, LANES), F32),
            pltpu.VMEM((n, rows, dv), BF16),
            pltpu.VMEM((n, rows, dv), BF16),
            pltpu.VMEM((nq * nt, dv), BF16),
            pltpu.VMEM((2, 8, LANES), F32),
            pltpu.VMEM((feat, dv), F32),
            pltpu.VMEM((n, piece, dv), F32),
            dma((2,)), dma((2,)),
        ]
        + [dma((n,))] * 8,
        compiler_params=pltpu.CompilerParams(
            collective_id=1, has_side_effects=True, vmem_limit_bytes=48 << 20
        ),
        name="grads",
    )(query_len, a_part, t_part, stat, pin, info, flat_h, proj)
    if not inside:
        gp = lax.psum(gp, "shard")
    return kl[0, :nq], gh.reshape(nq, nt, feat), gp


def solution(mesh):
    in_specs = (
        P("shard", None, "section"),
        P("section", None),
        P("shard", None, None),
        P("shard"),
        P("shard"),
        P("section", "shard", None, None),
        P("section", "shard", None),
        P("shard", "section"),
    )
    out_specs = (P("shard"), P("shard", None, "section"), P("section", None))
    return jax.shard_map(local, mesh=mesh, in_specs=in_specs, out_specs=out_specs, check_vma=False)
```
